32 devices in a mesh: pair: 2 (over core), ctx: 4 (over y, x), head: 4 (over z).
Axes of the slice: x: 2, y: 2, z: 4, core: 2. Of those that a mesh axis runs over, the one named last changes fastest.
Arguments:
- prompt_queries: bfloat16 [512, 8192], P(('pair', 'ctx'), 'head'), may hold values from -128 to 128
- prompt_key_rows: bfloat16 [512, 1024], P(('pair', 'ctx'), 'head'), may hold values from -8 to 8
- prompt_value_rows: bfloat16 [512, 1024], P(('pair', 'ctx'), 'head'), may hold values from -6 to 6
- answer_queries: bfloat16 [2, 256, 8192], P('pair', 'ctx', 'head'), may hold values from -128 to 128
- response_key_rows: bfloat16 [2, 256, 1024], P('pair', 'ctx', 'head'), may hold values from -8 to 8
- response_value_rows: bfloat16 [2, 256, 1024], P('pair', 'ctx', 'head'), may hold values from -6 to 6
- prompt_cotangent: bfloat16 [512, 8192], P(('pair', 'ctx'), 'head'), may hold values from -6 to 6
- answer_cotangent: bfloat16 [2, 256, 8192], P('pair', 'ctx', 'head'), may hold values from -6 to 6
- prompt_length: int32 [1], replicated, may hold values from 257 to 512
- answer_lengths: int32 [2], replicated, may hold values from 129 to 256
Outputs:
- prompt_attended: bfloat16 [512, 8192], P(('pair', 'ctx'), 'head')
- answer_attended: bfloat16 [2, 256, 8192], P('pair', 'ctx', 'head')
- prompt_query_grad: bfloat16 [512, 8192], P(('pair', 'ctx'), 'head')
- prompt_key_gradient: bfloat16 [512, 1024], P(('pair', 'ctx'), 'head')
- prompt_value_gradient: bfloat16 [512, 1024], P(('pair', 'ctx'), 'head')
- answer_query_grad: bfloat16 [2, 256, 8192], P('pair', 'ctx', 'head')
- response_key_gradient: bfloat16 [2, 256, 1024], P('pair', 'ctx', 'head')
- response_value_gradient: bfloat16 [2, 256, 1024], P('pair', 'ctx', 'head')
The draws below stay inside these ranges and needn't reach their ends.
All inputs are finite; a program needn't handle non-finite values.
Results may differ from the reference program's by a relative error of at most 0.0054.
Values may be sent and summed in bfloat16 or wider, within the bound.
A program may use at most 64 MiB of HBM per device.

```python
import jax
import jax.numpy as jnp
from jax import lax

QUERY_HEADS = 64
KEY_VALUE_HEADS = 8
HEAD_SIZE = 128
PROMPT_TOKENS = 512
RESPONSE_TOKENS = 256


def joint_draw(key):
    query_group_count = QUERY_HEADS // KEY_VALUE_HEADS
    prompt_key_input = jax.random.truncated_normal(jax.random.fold_in(key, 11), -5.0, 5.0, (PROMPT_TOKENS, KEY_VALUE_HEADS, HEAD_SIZE), jnp.float32)
    prompt_query_input = jax.random.truncated_normal(jax.random.fold_in(key, 12), -5.0, 5.0, (PROMPT_TOKENS, KEY_VALUE_HEADS, query_group_count, HEAD_SIZE), jnp.float32)
    response_key_input = jax.random.truncated_normal(jax.random.fold_in(key, 13), -5.0, 5.0, (2, RESPONSE_TOKENS, KEY_VALUE_HEADS, HEAD_SIZE), jnp.float32)
    response_query_input = jax.random.truncated_normal(jax.random.fold_in(key, 14), -5.0, 5.0, (2, RESPONSE_TOKENS, KEY_VALUE_HEADS, query_group_count, HEAD_SIZE), jnp.float32)
    return (prompt_query_input.reshape(PROMPT_TOKENS, QUERY_HEADS * HEAD_SIZE), prompt_key_input.reshape(PROMPT_TOKENS, KEY_VALUE_HEADS * HEAD_SIZE), response_query_input.reshape(2, RESPONSE_TOKENS, QUERY_HEADS * HEAD_SIZE), response_key_input.reshape(2, RESPONSE_TOKENS, KEY_VALUE_HEADS * HEAD_SIZE))


def draw_prompt_queries(key, part):
    return joint_draw(key)[0].astype(jnp.bfloat16)


def draw_prompt_key_rows(key, part):
    return joint_draw(key)[1].astype(jnp.bfloat16)


def draw_answer_queries(key, part):
    return joint_draw(key)[2].astype(jnp.bfloat16)


def draw_response_key_rows(key, part):
    return joint_draw(key)[3].astype(jnp.bfloat16)


def block_levels(own_key, shape, pieces, least, high):
    def one(axis_at, blocks):
        draws = jax.random.uniform(jax.random.fold_in(jax.random.fold_in(own_key, 6), axis_at), (blocks,), jnp.float32, least / len(pieces), high / len(pieces))
        return jnp.repeat(jnp.exp(draws), shape[axis_at] // blocks).reshape((-1,) + (1,) * (len(shape) - axis_at - 1))

    gain = one(*pieces[0])
    for cut in pieces[1:]:
        gain = gain * one(*cut)
    return gain


def gaussian(key, extent, spread, most, pieces=(), kind=jnp.bfloat16):
    loudness = block_levels(key, extent, pieces, -0.22, 0.18) if pieces else 1.0
    drawn = jax.random.normal(key, extent, jnp.float32) * spread * loudness
    return jnp.minimum(jnp.maximum(drawn, -most), most).astype(kind)


def setup_inputs(seed: int = 0) -> dict:
    seeds = jax.random.split(jax.random.key(seed), 11)
    return {
        "prompt_queries": draw_prompt_queries(jax.random.fold_in(seeds[10], 71), 0),
        "prompt_key_rows": draw_prompt_key_rows(jax.random.fold_in(seeds[10], 71), 0),
        "prompt_value_rows": gaussian(seeds[2], (PROMPT_TOKENS, KEY_VALUE_HEADS * HEAD_SIZE), 1.0, 6.0, ((0, 8), (1, 4))),
        "answer_queries": draw_answer_queries(jax.random.fold_in(seeds[10], 71), 0),
        "response_key_rows": draw_response_key_rows(jax.random.fold_in(seeds[10], 71), 0),
        "response_value_rows": gaussian(seeds[5], (2, RESPONSE_TOKENS, KEY_VALUE_HEADS * HEAD_SIZE), 1.0, 6.0, ((0, 2), (1, 4), (2, 4))),
        "prompt_cotangent": gaussian(seeds[6], (PROMPT_TOKENS, QUERY_HEADS * HEAD_SIZE), 1.0, 6.0, ((0, 8), (1, 4))),
        "answer_cotangent": gaussian(seeds[7], (2, RESPONSE_TOKENS, QUERY_HEADS * HEAD_SIZE), 1.0, 6.0, ((0, 2), (1, 4), (2, 4))),
        "prompt_length": jax.random.randint(seeds[8], (1,), PROMPT_TOKENS // 2 + 1, PROMPT_TOKENS + 1).astype(jnp.int32),
        "answer_lengths": jax.random.randint(seeds[9], (2,), RESPONSE_TOKENS // 2 + 1, RESPONSE_TOKENS + 1).astype(jnp.int32),
    }


NEGATIVE = -1.0e30


def attend(queries, cotangent, key_rows, value_rows, allowed, valid_rows, scaling):
    scores = jnp.dot(queries, key_rows.T, preferred_element_type=jnp.float32) * scaling
    scores = jnp.where(allowed, scores, NEGATIVE)
    row_max = jnp.max(scores, axis=1, keepdims=True)
    terms = jnp.where(allowed, jnp.exp(scores - row_max), 0.0)
    totals = jnp.sum(terms, axis=1, keepdims=True)
    log_total = row_max + jnp.log(totals)
    probs = terms.astype(jnp.bfloat16)
    output = jnp.dot(probs, value_rows, preferred_element_type=jnp.float32) / totals
    shares = jnp.where(allowed, jnp.exp(scores - log_total), 0.0)
    weights = shares.astype(jnp.bfloat16)
    attended = jnp.where(valid_rows[:, None], output, 0.0).astype(jnp.bfloat16)
    masked = jnp.where(valid_rows[:, None], cotangent, jnp.zeros_like(cotangent))
    row_delta = jnp.sum(masked.astype(jnp.float32) * output, axis=1, keepdims=True)
    prob_grad = jnp.dot(masked, value_rows.T, preferred_element_type=jnp.float32)
    score_grad = (shares * (prob_grad - row_delta)).astype(jnp.bfloat16)
    query_grad = (jnp.dot(score_grad, key_rows, preferred_element_type=jnp.float32) * scaling).astype(jnp.bfloat16)
    key_grad = jnp.dot(score_grad.T, queries, preferred_element_type=jnp.float32) * scaling
    value_grad = jnp.dot(weights.T, masked, preferred_element_type=jnp.float32)
    return attended, query_grad, key_grad, value_grad


def reference(prompt_queries, prompt_key_rows, prompt_value_rows, answer_queries, response_key_rows, response_value_rows, prompt_cotangent, answer_cotangent, prompt_length, answer_lengths):
    query_group_count = QUERY_HEADS // KEY_VALUE_HEADS
    scaling = HEAD_SIZE ** -0.5
    prompt_len = prompt_length[0]
    prompt_pos = jnp.arange(PROMPT_TOKENS, dtype=jnp.int32)
    answer_pos = jnp.arange(RESPONSE_TOKENS, dtype=jnp.int32)
    prompt_query_heads = prompt_queries.reshape(PROMPT_TOKENS, QUERY_HEADS, HEAD_SIZE).transpose(1, 0, 2)
    prompt_cot_heads = prompt_cotangent.reshape(PROMPT_TOKENS, QUERY_HEADS, HEAD_SIZE).transpose(1, 0, 2)
    answer_query_heads = answer_queries.reshape(2, RESPONSE_TOKENS, QUERY_HEADS, HEAD_SIZE).transpose(2, 0, 1, 3)
    answer_cot_heads = answer_cotangent.reshape(2, RESPONSE_TOKENS, QUERY_HEADS, HEAD_SIZE).transpose(2, 0, 1, 3)
    prompt_key_per_head = prompt_key_rows.reshape(PROMPT_TOKENS, KEY_VALUE_HEADS, HEAD_SIZE).transpose(1, 0, 2)
    prompt_value_per_head = prompt_value_rows.reshape(PROMPT_TOKENS, KEY_VALUE_HEADS, HEAD_SIZE).transpose(1, 0, 2)
    response_key_per_head = response_key_rows.reshape(2, RESPONSE_TOKENS, KEY_VALUE_HEADS, HEAD_SIZE).transpose(2, 0, 1, 3)
    response_value_per_head = response_value_rows.reshape(2, RESPONSE_TOKENS, KEY_VALUE_HEADS, HEAD_SIZE).transpose(2, 0, 1, 3)
    head_owner = jnp.arange(QUERY_HEADS, dtype=jnp.int32) // query_group_count
    causal = (prompt_pos[None, :] <= prompt_pos[:, None]) & (prompt_pos[None, :] < prompt_len)
    seen_prompt = jnp.broadcast_to((prompt_pos < prompt_len)[None, :], (RESPONSE_TOKENS, PROMPT_TOKENS))

    def per_head(inputs):
        queries, cotangent, later_queries, later_cot, owner = inputs
        key_rows = prompt_key_per_head[owner]
        value_rows = prompt_value_per_head[owner]
        first = attend(queries, cotangent, key_rows, value_rows, causal, prompt_pos < prompt_len, scaling)
        key_grad = first[2]
        value_grad = first[3]
        later = []
        for which in range(2):
            answer_len = answer_lengths[which]
            inner = (answer_pos[None, :] <= answer_pos[:, None]) & (answer_pos[None, :] < answer_len)
            joined_keys = jnp.concatenate([key_rows, response_key_per_head[owner, which]], axis=0)
            joined_values = jnp.concatenate([value_rows, response_value_per_head[owner, which]], axis=0)
            joined_allowed = jnp.concatenate([seen_prompt, inner], axis=1)
            result = attend(later_queries[which], later_cot[which], joined_keys, joined_values, joined_allowed, answer_pos < answer_len, scaling)
            key_grad = key_grad + result[2][:PROMPT_TOKENS]
            value_grad = value_grad + result[3][:PROMPT_TOKENS]
            later.append(result)
        answer_out = jnp.stack([later[0][0], later[1][0]])
        answer_qgrad = jnp.stack([later[0][1], later[1][1]])
        answer_kgrad = jnp.stack([later[0][2][PROMPT_TOKENS:], later[1][2][PROMPT_TOKENS:]])
        answer_vgrad = jnp.stack([later[0][3][PROMPT_TOKENS:], later[1][3][PROMPT_TOKENS:]])
        return first[0], first[1], key_grad, value_grad, answer_out, answer_qgrad, answer_kgrad, answer_vgrad

    output_collection = lax.map(per_head, (prompt_query_heads, prompt_cot_heads, answer_query_heads, answer_cot_heads, head_owner))
    prompt_attended = output_collection[0].transpose(1, 0, 2).reshape(PROMPT_TOKENS, QUERY_HEADS * HEAD_SIZE)
    prompt_query_grad = output_collection[1].transpose(1, 0, 2).reshape(PROMPT_TOKENS, QUERY_HEADS * HEAD_SIZE)
    prompt_key_gradient = output_collection[2].reshape(KEY_VALUE_HEADS, query_group_count, PROMPT_TOKENS, HEAD_SIZE).sum(axis=1).transpose(1, 0, 2).reshape(PROMPT_TOKENS, KEY_VALUE_HEADS * HEAD_SIZE).astype(jnp.bfloat16)
    prompt_value_gradient = output_collection[3].reshape(KEY_VALUE_HEADS, query_group_count, PROMPT_TOKENS, HEAD_SIZE).sum(axis=1).transpose(1, 0, 2).reshape(PROMPT_TOKENS, KEY_VALUE_HEADS * HEAD_SIZE).astype(jnp.bfloat16)
    answer_attended = output_collection[4].transpose(1, 2, 0, 3).reshape(2, RESPONSE_TOKENS, QUERY_HEADS * HEAD_SIZE)
    answer_query_grad = output_collection[5].transpose(1, 2, 0, 3).reshape(2, RESPONSE_TOKENS, QUERY_HEADS * HEAD_SIZE)
    response_key_gradient = output_collection[6].reshape(KEY_VALUE_HEADS, query_group_count, 2, RESPONSE_TOKENS, HEAD_SIZE).sum(axis=1).transpose(1, 2, 0, 3).reshape(2, RESPONSE_TOKENS, KEY_VALUE_HEADS * HEAD_SIZE).astype(jnp.bfloat16)
    response_value_gradient = output_collection[7].reshape(KEY_VALUE_HEADS, query_group_count, 2, RESPONSE_TOKENS, HEAD_SIZE).sum(axis=1).transpose(1, 2, 0, 3).reshape(2, RESPONSE_TOKENS, KEY_VALUE_HEADS * HEAD_SIZE).astype(jnp.bfloat16)
    return (prompt_attended, answer_attended, prompt_query_grad, prompt_key_gradient, prompt_value_gradient, answer_query_grad, response_key_gradient, response_value_gradient)
```

```python
import functools
import math

import jax
import jax.numpy as jnp
from jax import lax
from jax.experimental import pallas as pl
from jax.experimental.pallas import tpu as pltpu
from jax.sharding import PartitionSpec as P

KEY_VALUE_HEADS = 8
HEAD_SIZE = 128
NEGATIVE = -1e30
MESH = pl.DeviceIdType.MESH
F32 = jnp.float32
BF16 = jnp.bfloat16


def greet(pairs, ctxs, p, c):
    barrier = pltpu.get_barrier_semaphore()
    for e in range(1, pairs):
        pl.semaphore_signal(
            barrier, inc=1, device_id={"pair": lax.rem(p + e, pairs)}, device_id_type=MESH
        )
    for d in range(1, ctxs):
        pl.semaphore_signal(
            barrier, inc=1, device_id={"ctx": lax.rem(c + d, ctxs)}, device_id_type=MESH
        )
    pl.semaphore_wait(barrier, pairs + ctxs - 2)


def gather_kernel(pairs, ctxs, kp, vp, kr, vr, gp, gr, send_p, recv_p, send_r, recv_r, send_f, recv_f):
    p, c = lax.axis_index("pair"), lax.axis_index("ctx")
    own = p * ctxs + c
    gp[own, 0] = kp[...]
    gp[own, 1] = vp[...]
    gr[c, 0] = kr[0]
    gr[c, 1] = vr[0]
    greet(pairs, ctxs, p, c)

    def forward(slot, e, d):
        copy = pltpu.make_async_remote_copy(
            src_ref=gp.at[slot],
            dst_ref=gp.at[slot],
            send_sem=send_f.at[e - 1, d],
            recv_sem=recv_f.at[e - 1, d],
            device_id={"pair": lax.rem(p + e, pairs)},
            device_id_type=MESH,
        )
        copy.start()
        return copy

    across, replies, forwards = [], [], []
    for d in range(1, ctxs):
        copy = pltpu.make_async_remote_copy(
            src_ref=gp.at[own],
            dst_ref=gp.at[own],
            send_sem=send_p.at[d - 1],
            recv_sem=recv_p.at[d - 1],
            device_id={"ctx": lax.rem(c + d, ctxs)},
            device_id_type=MESH,
        )
        copy.start()
        across.append(copy)
    for d in range(1, ctxs):
        copy = pltpu.make_async_remote_copy(
            src_ref=gr.at[c],
            dst_ref=gr.at[c],
            send_sem=send_r.at[d - 1],
            recv_sem=recv_r.at[d - 1],
            device_id={"ctx": lax.rem(c + d, ctxs)},
            device_id_type=MESH,
        )
        copy.start()
        replies.append(copy)
    for e in range(1, pairs):
        forwards.append(forward(own, e, 0))
    for d in range(1, ctxs):
        across[d - 1].wait_recv()
        slot = p * ctxs + lax.rem(c + ctxs - d, ctxs)
        for e in range(1, pairs):
            forwards.append(forward(slot, e, d))
    for copy in across:
        copy.wait_send()
    for copy in replies + forwards:
        copy.wait()


def gather(pairs, ctxs, kp, vp, kr, vr):
    rows, width = kp.shape
    vmem = pl.BlockSpec(memory_space=pltpu.VMEM)
    return pl.pallas_call(
        functools.partial(gather_kernel, pairs, ctxs),
        out_shape=(
            jax.ShapeDtypeStruct((pairs * ctxs, 2, rows, width), BF16),
            jax.ShapeDtypeStruct((ctxs, 2, kr.shape[1], width), BF16),
        ),
        in_specs=[vmem] * 4,
        out_specs=(vmem, vmem),
        scratch_shapes=[
            pltpu.SemaphoreType.DMA((ctxs - 1,)),
            pltpu.SemaphoreType.DMA((ctxs - 1,)),
            pltpu.SemaphoreType.DMA((ctxs - 1,)),
            pltpu.SemaphoreType.DMA((ctxs - 1,)),
            pltpu.SemaphoreType.DMA((pairs - 1, ctxs)),
            pltpu.SemaphoreType.DMA((pairs - 1, ctxs)),
        ],
        compiler_params=pltpu.CompilerParams(
            collective_id=0, has_side_effects=True, vmem_limit_bytes=32 * 2**20
        ),
    )(kp, vp, kr, vr)


def reduce_kernel(
    pairs, ctxs, tp, tr, kp, vp, kr, vr, from_pair, from_ctx, from_reply, summed,
    send_f, recv_f, send_p, recv_p, send_r, recv_r,
):
    p, c = lax.axis_index("pair"), lax.axis_index("ctx")
    own = p * ctxs + c
    greet(pairs, ctxs, p, c)
    inner, across, replies = [], [], []
    for d in list(range(1, ctxs)) + [0]:
        for e in range(1, pairs):
            q = lax.rem(p + e, pairs)
            copy = pltpu.make_async_remote_copy(
                src_ref=tp.at[q * ctxs + lax.rem(c + d, ctxs)],
                dst_ref=from_pair.at[e - 1, d],
                send_sem=send_f.at[e - 1, d],
                recv_sem=recv_f.at[e - 1, d],
                device_id={"pair": q},
                device_id_type=MESH,
            )
            copy.start()
            inner.append((d, e, copy))
    for d in range(1, ctxs):
        peer = lax.rem(c + d, ctxs)
        copy = pltpu.make_async_remote_copy(
            src_ref=tr.at[peer],
            dst_ref=from_reply.at[d - 1],
            send_sem=send_r.at[d - 1],
            recv_sem=recv_r.at[d - 1],
            device_id={"ctx": peer},
            device_id_type=MESH,
        )
        copy.start()
        replies.append(copy)

    def pair_sum(d, which):
        total = tp[p * ctxs + lax.rem(c + d, ctxs), which].astype(F32)
        for e in range(1, pairs):
            total = total + from_pair[e - 1, d, which].astype(F32)
        return total

    for d in range(1, ctxs):
        for at, _, copy in inner:
            if at == d:
                copy.wait_recv()
        for which in range(2):
            summed[d - 1, which] = pair_sum(d, which).astype(BF16)
        copy = pltpu.make_async_remote_copy(
            src_ref=summed.at[d - 1],
            dst_ref=from_ctx.at[d - 1],
            send_sem=send_p.at[d - 1],
            recv_sem=recv_p.at[d - 1],
            device_id={"ctx": lax.rem(c + d, ctxs)},
            device_id_type=MESH,
        )
        copy.start()
        across.append(copy)
    for at, _, copy in inner:
        if at == 0:
            copy.wait_recv()
    for copy in replies:
        copy.wait_recv()
    for which, out in ((0, kr), (1, vr)):
        total = tr[c, which].astype(F32)
        for d in range(1, ctxs):
            total = total + from_reply[d - 1, which].astype(F32)
        out[0] = total.astype(BF16)
    for copy in across:
        copy.wait_recv()
    for which, out in ((0, kp), (1, vp)):
        total = pair_sum(0, which)
        for d in range(1, ctxs):
            total = total + from_ctx[d - 1, which].astype(F32)
        out[...] = total.astype(BF16)
    for _, _, copy in inner:
        copy.wait_send()
    for copy in across + replies:
        copy.wait_send()


def reduce(pairs, ctxs, tp, tr):
    _, _, rows, width = tp.shape
    later = tr.shape[2]
    vmem = pl.BlockSpec(memory_space=pltpu.VMEM)
    return pl.pallas_call(
        functools.partial(reduce_kernel, pairs, ctxs),
        out_shape=(
            jax.ShapeDtypeStruct((rows, width), BF16),
            jax.ShapeDtypeStruct((rows, width), BF16),
            jax.ShapeDtypeStruct((1, later, width), BF16),
            jax.ShapeDtypeStruct((1, later, width), BF16),
        ),
        in_specs=[vmem] * 2,
        out_specs=(vmem,) * 4,
        scratch_shapes=[
            pltpu.VMEM((pairs - 1, ctxs, 2, rows, width), BF16),
            pltpu.VMEM((ctxs - 1, 2, rows, width), BF16),
            pltpu.VMEM((ctxs - 1, 2, later, width), BF16),
            pltpu.VMEM((ctxs - 1, 2, rows, width), BF16),
            pltpu.SemaphoreType.DMA((pairs - 1, ctxs)),
            pltpu.SemaphoreType.DMA((pairs - 1, ctxs)),
            pltpu.SemaphoreType.DMA((ctxs - 1,)),
            pltpu.SemaphoreType.DMA((ctxs - 1,)),
            pltpu.SemaphoreType.DMA((ctxs - 1,)),
            pltpu.SemaphoreType.DMA((ctxs - 1,)),
        ],
        compiler_params=pltpu.CompilerParams(
            collective_id=1, has_side_effects=True, vmem_limit_bytes=32 * 2**20
        ),
    )(tp, tr)


def dot(a, b):
    return lax.dot_general(a, b, (((1,), (0,)), ((), ())), preferred_element_type=F32)


def dot_nt(a, b):
    return lax.dot_general(a, b, (((1,), (1,)), ((), ())), preferred_element_type=F32)


def row_positions(first, count, rows):
    lane = lax.broadcasted_iota(jnp.int32, (1, count), 1)
    return first + lax.rem(lane, jnp.int32(rows))


def attend_block(parts, queries, cotangent, valid, scaling, grads):
    factor = scaling * math.log2(math.e)
    scores = []
    top = None
    for keys, _, _, _, limit in parts:
        s = dot_nt(keys, queries)
        at = lax.broadcasted_iota(jnp.int32, s.shape, 0)
        s = jnp.where(at <= limit, s, NEGATIVE)
        m = jnp.max(s, axis=0, keepdims=True)
        top = m if top is None else jnp.maximum(top, m)
        scores.append(s)
    terms = [jnp.exp2((s - top) * factor) for s in scores]
    total = sum(jnp.sum(t, axis=0, keepdims=True) for t in terms)
    inverse = 1.0 / total
    output = sum(dot(part[3], t.astype(BF16)) for part, t in zip(parts, terms))
    output = jnp.where(valid, output * inverse, 0.0).astype(BF16)
    prob_grads = [dot_nt(part[1], cotangent) for part in parts]
    shares = [t * inverse for t in terms]
    delta = sum(jnp.sum(w * g, axis=0, keepdims=True) for w, g in zip(shares, prob_grads))
    query_grad = None
    for part, w, g, (key_grad, value_grad, fresh) in zip(parts, shares, prob_grads, grads):
        value_add = dot(w.astype(BF16), cotangent)
        score_grad = (w * (g - delta)).astype(BF16)
        key_add = dot(score_grad, queries)
        if fresh:
            value_grad[...] = value_add
            key_grad[...] = key_add
        else:
            value_grad[...] += value_add
            key_grad[...] += key_add
        add = dot(part[2], score_grad)
        query_grad = add if query_grad is None else query_grad + add
    return output, (query_grad * scaling).astype(BF16)


def attend_kernel(
    pairs, ctxs, plen, alen, gp, gr, q, aq, do, ado,
    out, aout, dq, adq, tp, tr,
    kgrad, vgrad, kgrad_r, vgrad_r,
):
    p, c = lax.axis_index("pair"), lax.axis_index("ctx")
    slots, _, rows, size = gp.shape
    later = gr.shape[2]
    group = q.shape[1] // size
    scaling = size ** (-0.5)
    prompt_len = plen[0]
    answer_len = alen[p]
    prompt_first = (p * ctxs + c) * rows
    answer_first = c * later

    keys = gp[:, 0].reshape(slots * rows, size)
    values = gp[:, 1].reshape(slots * rows, size)
    keys_r = gr[:, 0].reshape(ctxs * later, size)
    values_r = gr[:, 1].reshape(ctxs * later, size)
    keys_t, values_t = keys.T, values.T
    keys_rt, values_rt = keys_r.T, values_r.T

    def stacked(ref, heads):
        return jnp.concatenate([ref[:, h * size : (h + 1) * size] for h in heads], axis=0)

    for answer in (False, True):
        count = later if answer else rows
        per_block = max(1, 256 // count)
        first = answer_first if answer else prompt_first
        live = answer_len if answer else prompt_len
        for start in range(0, group, per_block):
            heads = list(range(start, min(group, start + per_block)))
            lanes = len(heads) * count
            pos = row_positions(first, lanes, count)
            valid = pos < live
            queries = stacked(aq if answer else q, heads)
            cotangent = stacked(ado if answer else do, heads)
            live_row = (
                first
                + lax.rem(lax.broadcasted_iota(jnp.int32, cotangent.shape, 0), jnp.int32(count))
                < live
            )
            cotangent = jnp.where(live_row, cotangent.astype(F32), 0.0).astype(BF16)
            limit = jnp.minimum(pos, live - 1)
            if answer:
                parts = [
                    (keys, values, keys_t, values_t, jnp.full((1, lanes), prompt_len - 1, jnp.int32)),
                    (keys_r, values_r, keys_rt, values_rt, limit),
                ]
                grads = [(kgrad, vgrad, False), (kgrad_r, vgrad_r, start == 0)]
            else:
                parts = [(keys, values, keys_t, values_t, limit)]
                grads = [(kgrad, vgrad, start == 0)]
            o, g = attend_block(parts, queries, cotangent, valid, scaling, grads)
            o, g = o.T, g.T
            for i, h in enumerate(heads):
                cut, cols = slice(i * count, (i + 1) * count), slice(h * size, (h + 1) * size)
                (aout if answer else out)[:, cols] = o[cut]
                (adq if answer else dq)[:, cols] = g[cut]
    tp[:, 0] = (kgrad[...] * scaling).astype(BF16).reshape(slots, rows, size)
    tp[:, 1] = vgrad[...].astype(BF16).reshape(slots, rows, size)
    tr[:, 0] = (kgrad_r[...] * scaling).astype(BF16).reshape(ctxs, later, size)
    tr[:, 1] = vgrad_r[...].astype(BF16).reshape(ctxs, later, size)


def attend(pairs, ctxs, gp, gr, q, aq, do, ado, plen, alen):
    size = HEAD_SIZE
    slots, _, rows, width = gp.shape
    later = gr.shape[2]
    heads = width // size
    cols = q.shape[1] // heads
    smem = pl.BlockSpec(memory_space=pltpu.SMEM)
    kv = pl.BlockSpec((slots, 2, rows, size), lambda h: (0, 0, 0, h))
    kv_r = pl.BlockSpec((ctxs, 2, later, size), lambda h: (0, 0, 0, h))
    flat = pl.BlockSpec((rows, cols), lambda h: (0, h))
    deep = pl.BlockSpec((None, later, cols), lambda h: (0, 0, h))
    return pl.pallas_call(
        functools.partial(attend_kernel, pairs, ctxs),
        grid=(heads,),
        out_shape=(
            jax.ShapeDtypeStruct(q.shape, BF16),
            jax.ShapeDtypeStruct(aq.shape, BF16),
            jax.ShapeDtypeStruct(q.shape, BF16),
            jax.ShapeDtypeStruct(aq.shape, BF16),
            jax.ShapeDtypeStruct(gp.shape, BF16),
            jax.ShapeDtypeStruct(gr.shape, BF16),
        ),
        in_specs=[smem, smem, kv, kv_r, flat, deep, flat, deep],
        out_specs=(flat, deep, flat, deep, kv, kv_r),
        scratch_shapes=[
            pltpu.VMEM((slots * rows, size), F32),
            pltpu.VMEM((slots * rows, size), F32),
            pltpu.VMEM((ctxs * later, size), F32),
            pltpu.VMEM((ctxs * later, size), F32),
        ],
        compiler_params=pltpu.CompilerParams(vmem_limit_bytes=56 * 2**20),
    )(plen, alen, gp, gr, q, aq, do, ado)


def body(pairs, ctxs, q, kp, vp, aq, kr, vr, do, ado, plen, alen):
    gp, gr = gather(pairs, ctxs, kp, vp, kr, vr)
    out, aout, dq, adq, tp, tr = attend(pairs, ctxs, gp, gr, q, aq, do, ado, plen, alen)
    dkp, dvp, dkr, dvr = reduce(pairs, ctxs, tp, tr)
    return out, aout, dq, dkp, dvp, adq, dkr, dvr


def solution(mesh):
    flat = P(("pair", "ctx"), "head")
    deep = P("pair", "ctx", "head")
    return jax.shard_map(
        functools.partial(body, mesh.shape["pair"], mesh.shape["ctx"]),
        mesh=mesh,
        in_specs=(flat, flat, flat, deep, deep, deep, flat, deep, P(), P()),
        out_specs=(flat, deep, flat, flat, flat, deep, deep, deep),
        check_vma=False,
    )
```

```python
import functools
import math

import jax
import jax.numpy as jnp
from jax import lax
from jax.experimental import pallas as pl
from jax.experimental.pallas import tpu as pltpu
from jax.sharding import PartitionSpec as P

KEY_VALUE_HEADS = 8
HEAD_SIZE = 128
NEGATIVE = -1e30
MESH = pl.DeviceIdType.MESH
F32 = jnp.float32
BF16 = jnp.bfloat16


def greet(pairs, ctxs, p, c):
    barrier = pltpu.get_barrier_semaphore()
    for e in range(1, pairs):
        pl.semaphore_signal(
            barrier, inc=1, device_id={"pair": lax.rem(p + e, pairs)}, device_id_type=MESH
        )
    for d in range(1, ctxs):
        pl.semaphore_signal(
            barrier, inc=1, device_id={"ctx": lax.rem(c + d, ctxs)}, device_id_type=MESH
        )
    pl.semaphore_wait(barrier, pairs + ctxs - 2)


def dot(a, b):
    return lax.dot_general(a, b, (((1,), (0,)), ((), ())), preferred_element_type=F32)


def dot_nt(a, b):
    return lax.dot_general(a, b, (((1,), (1,)), ((), ())), preferred_element_type=F32)


def row_positions(first, count, rows):
    lane = lax.broadcasted_iota(jnp.int32, (1, count), 1)
    return first + lax.rem(lane, jnp.int32(rows))


def attend_block(parts, queries, cotangent, valid, scaling, grads):
    factor = scaling * math.log2(math.e)
    scores = []
    top = None
    for keys, _, _, _, limit in parts:
        s = dot_nt(keys, queries)
        at = lax.broadcasted_iota(jnp.int32, s.shape, 0)
        s = jnp.where(at <= limit, s, NEGATIVE)
        m = jnp.max(s, axis=0, keepdims=True)
        top = m if top is None else jnp.maximum(top, m)
        scores.append(s)
    terms = [jnp.exp2((s - top) * factor) for s in scores]
    total = sum(jnp.sum(t, axis=0, keepdims=True) for t in terms)
    inverse = 1.0 / total
    output = sum(dot(part[3], t.astype(BF16)) for part, t in zip(parts, terms))
    output = jnp.where(valid, output * inverse, 0.0).astype(BF16)
    prob_grads = [dot_nt(part[1], cotangent) for part in parts]
    shares = [t * inverse for t in terms]
    delta = sum(jnp.sum(w * g, axis=0, keepdims=True) for w, g in zip(shares, prob_grads))
    query_grad = None
    for part, w, g, (key_grad, value_grad, fresh) in zip(parts, shares, prob_grads, grads):
        value_add = dot(w.astype(BF16), cotangent)
        score_grad = (w * (g - delta)).astype(BF16)
        key_add = dot(score_grad, queries)
        if fresh:
            value_grad[...] = value_add
            key_grad[...] = key_add
        else:
            value_grad[...] += value_add
            key_grad[...] += key_add
        add = dot(part[2], score_grad)
        query_grad = add if query_grad is None else query_grad + add
    return output, (query_grad * scaling).astype(BF16)


def remote(src, dst, send, recv, device):
    copy = pltpu.make_async_remote_copy(
        src_ref=src, dst_ref=dst, send_sem=send, recv_sem=recv, device_id=device, device_id_type=MESH
    )
    copy.start()
    return copy


def fused_kernel(
    pairs, ctxs, kv_heads,
    plen, alen, q, kp, vp, aq, kr, vr, do, ado,
    out, aout, dq, dkp, dvp, adq, dkr, dvr,
    gp, gr, q_v, aq_v, do_v, ado_v, out_v, aout_v, dq_v, adq_v,
    kgrad, vgrad, kgrad_r, vgrad_r, tp, tr, from_pair, from_ctx, from_reply, summed, done_p, done_r,
    load_sem, store_sem,
    g_send, g_recv, r_send, r_recv, f_send, f_recv,
    x_send, x_recv, y_send, y_recv, z_send, z_recv,
):
    p, c = lax.axis_index("pair"), lax.axis_index("ctx")
    own = p * ctxs + c
    slots = pairs * ctxs
    rows, later, size = q.shape[0], aq.shape[1], HEAD_SIZE
    cols = q.shape[1] // kv_heads
    group = cols // size
    scaling = size ** (-0.5)
    every = range(kv_heads)

    def peer(d):
        return lax.rem(c + d, ctxs)

    def partner(e):
        return lax.rem(p + e, pairs)

    loads = {}

    def load(h, index, src, dst):
        copy = pltpu.make_async_copy(src, dst, load_sem.at[h, index])
        copy.start()
        loads[h, index] = copy

    for h in every:
        narrow = pl.ds(h * size, size)
        load(h, 0, kp.at[:, narrow], gp.at[h, own, 0])
        load(h, 1, vp.at[:, narrow], gp.at[h, own, 1])
        load(h, 2, kr.at[0, :, narrow], gr.at[h, c, 0])
        load(h, 3, vr.at[0, :, narrow], gr.at[h, c, 1])
    for h in every:
        wide = pl.ds(h * cols, cols)
        load(h, 4, q.at[:, wide], q_v.at[h])
        load(h, 5, do.at[:, wide], do_v.at[h])
        load(h, 6, aq.at[0, :, wide], aq_v.at[h])
        load(h, 7, ado.at[0, :, wide], ado_v.at[h])
    greet(pairs, ctxs, p, c)

    across = {h: [] for h in every}
    replies = {h: [] for h in every}
    forwards = {h: [] for h in every}
    for h in every:
        for i in range(4):
            loads[h, i].wait()
        for d in range(1, ctxs):
            own_slot = gp.at[h, own]
            across[h].append(
                remote(own_slot, own_slot, g_send.at[h, d - 1], g_recv.at[h, d - 1], {"ctx": peer(d)})
            )
        for e in range(1, pairs):
            own_slot = gp.at[h, own]
            forwards[h].append(
                remote(own_slot, own_slot, f_send.at[h, e - 1, 0], f_recv.at[h, e - 1, 0], {"pair": partner(e)})
            )
        for d in range(1, ctxs):
            reply = gr.at[h, c]
            replies[h].append(
                remote(reply, reply, r_send.at[h, d - 1], r_recv.at[h, d - 1], {"ctx": peer(d)})
            )

    def forward(h):
        for d in range(1, ctxs):
            across[h][d - 1].wait_recv()
            slot = gp.at[h, p * ctxs + lax.rem(c + ctxs - d, ctxs)]
            for e in range(1, pairs):
                forwards[h].append(
                    remote(slot, slot, f_send.at[h, e - 1, d], f_recv.at[h, e - 1, d], {"pair": partner(e)})
                )

    inner = {h: [] for h in every}
    outer = {h: [] for h in every}
    back = {h: [] for h in every}

    def send_terms(h):
        for d in list(range(1, ctxs)) + [0]:
            for e in range(1, pairs):
                inner[h].append((d, remote(
                    tp.at[h, partner(e) * ctxs + peer(d)], from_pair.at[h, e - 1, d],
                    x_send.at[h, e - 1, d], x_recv.at[h, e - 1, d], {"pair": partner(e)},
                )))
        for d in range(1, ctxs):
            back[h].append(remote(
                tr.at[h, peer(d)], from_reply.at[h, d - 1],
                z_send.at[h, d - 1], z_recv.at[h, d - 1], {"ctx": peer(d)},
            ))

    def pair_sum(h, d):
        total = tp[h, p * ctxs + peer(d)].astype(F32)
        for e in range(1, pairs):
            total = total + from_pair[h, e - 1, d].astype(F32)
        return total

    def pass_on(h):
        for d in range(1, ctxs):
            for at, copy in inner[h]:
                if at == d:
                    copy.wait_recv()
            summed[h, d - 1] = pair_sum(h, d).astype(BF16)
            outer[h].append(remote(
                summed.at[h, d - 1], from_ctx.at[h, d - 1],
                y_send.at[h, d - 1], y_recv.at[h, d - 1], {"ctx": peer(d)},
            ))

    stores = []

    def store(h, index, src, dst):
        copy = pltpu.make_async_copy(src, dst, store_sem.at[h, index])
        copy.start()
        stores.append(copy)

    def finish(h):
        narrow = pl.ds(h * size, size)
        for copy in back[h]:
            copy.wait_recv()
        total = tr[h, c].astype(F32)
        for d in range(1, ctxs):
            total = total + from_reply[h, d - 1].astype(F32)
        done_r[h] = total.astype(BF16)
        store(h, 4, done_r.at[h, 0], dkr.at[0, :, narrow])
        store(h, 5, done_r.at[h, 1], dvr.at[0, :, narrow])
        for at, copy in inner[h]:
            if at == 0:
                copy.wait_recv()
        total = pair_sum(h, 0)
        for d in range(1, ctxs):
            outer[h][d - 1].wait_recv()
            total = total + from_ctx[h, d - 1].astype(F32)
        done_p[h] = total.astype(BF16)
        store(h, 6, done_p.at[h, 0], dkp.at[:, narrow])
        store(h, 7, done_p.at[h, 1], dvp.at[:, narrow])

    prompt_len = plen[0]
    answer_len = alen[p]
    prompt_first = own * rows
    answer_first = c * later

    def stacked(ref, h, heads):
        return jnp.concatenate([ref[h, :, i * size : (i + 1) * size] for i in heads], axis=0)

    forward(0)
    for h in every:
        for copy in forwards[h] + replies[h]:
            copy.wait_recv()
        keys = gp[h, :, 0].reshape(slots * rows, size)
        values = gp[h, :, 1].reshape(slots * rows, size)
        keys_r = gr[h, :, 0].reshape(ctxs * later, size)
        values_r = gr[h, :, 1].reshape(ctxs * later, size)
        keys_t, values_t = keys.T, values.T
        keys_rt, values_rt = keys_r.T, values_r.T
        for i in range(4, 8):
            loads[h, i].wait()
        for answer in (False, True):
            count = later if answer else rows
            per_block = max(1, 256 // count)
            first = answer_first if answer else prompt_first
            live = answer_len if answer else prompt_len
            for start in range(0, group, per_block):
                heads = list(range(start, min(group, start + per_block)))
                lanes = len(heads) * count
                pos = row_positions(first, lanes, count)
                queries = stacked(aq_v if answer else q_v, h, heads)
                cotangent = stacked(ado_v if answer else do_v, h, heads)
                live_row = (
                    first
                    + lax.rem(lax.broadcasted_iota(jnp.int32, cotangent.shape, 0), jnp.int32(count))
                    < live
                )
                cotangent = jnp.where(live_row, cotangent.astype(F32), 0.0).astype(BF16)
                limit = jnp.minimum(pos, live - 1)
                if answer:
                    whole = jnp.full((1, lanes), prompt_len - 1, jnp.int32)
                    parts = [
                        (keys, values, keys_t, values_t, whole),
                        (keys_r, values_r, keys_rt, values_rt, limit),
                    ]
                    grads = [(kgrad, vgrad, False), (kgrad_r, vgrad_r, start == 0)]
                else:
                    parts = [(keys, values, keys_t, values_t, limit)]
                    grads = [(kgrad, vgrad, start == 0)]
                o, g = attend_block(parts, queries, cotangent, pos < live, scaling, grads)
                o, g = o.T, g.T
                for i, k in enumerate(heads):
                    cut, at = slice(i * count, (i + 1) * count), slice(k * size, (k + 1) * size)
                    (aout_v if answer else out_v)[h, :, at] = o[cut]
                    (adq_v if answer else dq_v)[h, :, at] = g[cut]
                if not answer and start == 0:
                    if h > 0:
                        pass_on(h - 1)
                    if h + 1 < kv_heads:
                        forward(h + 1)
        tp[h, :, 0] = (kgrad[...] * scaling).astype(BF16).reshape(slots, rows, size)
        tp[h, :, 1] = vgrad[...].astype(BF16).reshape(slots, rows, size)
        tr[h, :, 0] = (kgrad_r[...] * scaling).astype(BF16).reshape(ctxs, later, size)
        tr[h, :, 1] = vgrad_r[...].astype(BF16).reshape(ctxs, later, size)
        send_terms(h)
        wide = pl.ds(h * cols, cols)
        store(h, 0, out_v.at[h], out.at[:, wide])
        store(h, 1, dq_v.at[h], dq.at[:, wide])
        store(h, 2, aout_v.at[h], aout.at[0, :, wide])
        store(h, 3, adq_v.at[h], adq.at[0, :, wide])
        if h > 0:
            finish(h - 1)
    pass_on(kv_heads - 1)
    finish(kv_heads - 1)
    for h in every:
        for copy in across[h] + forwards[h] + replies[h] + outer[h] + back[h]:
            copy.wait_send()
        for _, copy in inner[h]:
            copy.wait_send()
    for copy in stores:
        copy.wait()


def fused(pairs, ctxs, q, kp, vp, aq, kr, vr, do, ado, plen, alen):
    size = HEAD_SIZE
    rows, width = kp.shape
    later = kr.shape[1]
    heads = width // size
    cols = q.shape[1] // heads
    slots = pairs * ctxs
    smem = pl.BlockSpec(memory_space=pltpu.SMEM)
    hbm = pl.BlockSpec(memory_space=pltpu.HBM)
    dma = pltpu.SemaphoreType.DMA
    like = lambda x: jax.ShapeDtypeStruct(x.shape, BF16)
    wide = pltpu.VMEM((heads, rows, cols), BF16)
    wide_r = pltpu.VMEM((heads, later, cols), BF16)
    terms = pltpu.VMEM((heads, slots, 2, rows, size), BF16)
    terms_r = pltpu.VMEM((heads, ctxs, 2, later, size), BF16)
    return pl.pallas_call(
        functools.partial(fused_kernel, pairs, ctxs, heads),
        out_shape=tuple(map(like, (q, aq, q, kp, vp, aq, kr, vr))),
        in_specs=[smem] * 2 + [hbm] * 8,
        out_specs=(hbm,) * 8,
        scratch_shapes=[
            terms, terms_r, wide, wide_r, wide, wide_r, wide, wide_r, wide, wide_r,
            pltpu.VMEM((slots * rows, size), F32),
            pltpu.VMEM((slots * rows, size), F32),
            pltpu.VMEM((ctxs * later, size), F32),
            pltpu.VMEM((ctxs * later, size), F32),
            terms, terms_r,
            pltpu.VMEM((heads, pairs - 1, ctxs, 2, rows, size), BF16),
            pltpu.VMEM((heads, ctxs - 1, 2, rows, size), BF16),
            pltpu.VMEM((heads, ctxs - 1, 2, later, size), BF16),
            pltpu.VMEM((heads, ctxs - 1, 2, rows, size), BF16),
            pltpu.VMEM((heads, 2, rows, size), BF16),
            pltpu.VMEM((heads, 2, later, size), BF16),
            dma((heads, 8)), dma((heads, 8)),
            dma((heads, ctxs - 1)), dma((heads, ctxs - 1)),
            dma((heads, ctxs - 1)), dma((heads, ctxs - 1)),
            dma((heads, pairs - 1, ctxs)), dma((heads, pairs - 1, ctxs)),
            dma((heads, pairs - 1, ctxs)), dma((heads, pairs - 1, ctxs)),
            dma((heads, ctxs - 1)), dma((heads, ctxs - 1)),
            dma((heads, ctxs - 1)), dma((heads, ctxs - 1)),
        ],
        compiler_params=pltpu.CompilerParams(
            collective_id=0, has_side_effects=True, vmem_limit_bytes=56 * 2**20
        ),
    )(plen, alen, q, kp, vp, aq, kr, vr, do, ado)


def hand_on_kernel(count, *refs):
    sems = refs[-1]
    copies = [
        pltpu.make_async_copy(refs[i], refs[count + i], sems.at[i]) for i in range(count)
    ]
    for copy in copies:
        copy.start()
    for copy in copies:
        copy.wait()


def hand_on(arrays):
    hbm = pl.BlockSpec(memory_space=pltpu.HBM)
    count = len(arrays)
    return pl.pallas_call(
        functools.partial(hand_on_kernel, count),
        out_shape=tuple(jax.ShapeDtypeStruct(x.shape, x.dtype) for x in arrays),
        in_specs=[hbm] * count,
        out_specs=(hbm,) * count,
        scratch_shapes=[pltpu.SemaphoreType.DMA((count,))],
    )(*arrays)


def body(pairs, ctxs, *operands):
    return hand_on(fused(pairs, ctxs, *operands))


def solution(mesh):
    flat = P(("pair", "ctx"), "head")
    deep = P("pair", "ctx", "head")
    return jax.shard_map(
        functools.partial(body, mesh.shape["pair"], mesh.shape["ctx"]),
        mesh=mesh,
        in_specs=(flat, flat, flat, deep, deep, deep, flat, deep, P(), P()),
        out_specs=(flat, deep, flat, flat, flat, deep, deep, deep),
        check_vma=False,
    )
```

```python
import functools
import math

import jax
import jax.numpy as jnp
from jax import lax
from jax.experimental import pallas as pl
from jax.experimental.pallas import tpu as pltpu
from jax.sharding import PartitionSpec as P

KEY_VALUE_HEADS = 8
HEAD_SIZE = 128
NEGATIVE = -1e30
MESH = pl.DeviceIdType.MESH
F32 = jnp.float32
BF16 = jnp.bfloat16


def greet(pairs, ctxs, p, c):
    barrier = pltpu.get_barrier_semaphore()
    for e in range(1, pairs):
        pl.semaphore_signal(
            barrier, inc=1, device_id={"pair": lax.rem(p + e, pairs)}, device_id_type=MESH
        )
    for d in range(1, ctxs):
        pl.semaphore_signal(
            barrier, inc=1, device_id={"ctx": lax.rem(c + d, ctxs)}, device_id_type=MESH
        )
    pl.semaphore_wait(barrier, pairs + ctxs - 2)


def dot(a, b):
    return lax.dot_general(a, b, (((1,), (0,)), ((), ())), preferred_element_type=F32)


def dot_nt(a, b):
    return lax.dot_general(a, b, (((1,), (1,)), ((), ())), preferred_element_type=F32)


def row_positions(first, count, rows):
    lane = lax.broadcasted_iota(jnp.int32, (1, count), 1)
    return first + lax.rem(lane, jnp.int32(rows))


def attend_block(parts, queries, cotangent, valid, scaling, grads):
    factor = scaling * math.log2(math.e)
    scores = []
    top = None
    for keys, _, _, _, limit in parts:
        s = dot_nt(keys, queries)
        at = lax.broadcasted_iota(jnp.int32, s.shape, 0)
        s = jnp.where(at <= limit, s, NEGATIVE)
        m = jnp.max(s, axis=0, keepdims=True)
        top = m if top is None else jnp.maximum(top, m)
        scores.append(s)
    terms = [jnp.exp2((s - top) * factor) for s in scores]
    total = sum(jnp.sum(t, axis=0, keepdims=True) for t in terms)
    inverse = 1.0 / total
    output = sum(dot(part[3], t.astype(BF16)) for part, t in zip(parts, terms))
    output = jnp.where(valid, output * inverse, 0.0).astype(BF16)
    prob_grads = [dot_nt(part[1], cotangent) for part in parts]
    shares = [t * inverse for t in terms]
    delta = sum(jnp.sum(w * g, axis=0, keepdims=True) for w, g in zip(shares, prob_grads))
    query_grad = None
    for part, w, g, (key_grad, value_grad, fresh) in zip(parts, shares, prob_grads, grads):
        value_add = dot(w.astype(BF16), cotangent)
        score_grad = (w * (g - delta)).astype(BF16)
        key_add = dot(score_grad, queries)
        if fresh:
            value_grad[...] = value_add
            key_grad[...] = key_add
        else:
            value_grad[...] += value_add
            key_grad[...] += key_add
        add = dot(part[2], score_grad)
        query_grad = add if query_grad is None else query_grad + add
    return output, (query_grad * scaling).astype(BF16)


def remote(src, dst, send, recv, device):
    copy = pltpu.make_async_remote_copy(
        src_ref=src, dst_ref=dst, send_sem=send, recv_sem=recv, device_id=device, device_id_type=MESH
    )
    copy.start()
    return copy


def fused_kernel(
    pairs, ctxs, kv_heads,
    plen, alen, q, kp, vp, aq, kr, vr, do, ado,
    out_h, aout_h, dq_h, dkp_h, dvp_h, adq_h, dkr_h, dvr_h,
    gp, gr, q_v, aq_v, do_v, ado_v,
    out, aout, dq, dkp, dvp, adq, dkr, dvr,
    kgrad, vgrad, kgrad_r, vgrad_r, tp, tr, from_pair, from_ctx, from_reply, summed,
    load_sem, store_sem,
    g_send, g_recv, r_send, r_recv, f_send, f_recv,
    x_send, x_recv, y_send, y_recv, z_send, z_recv,
):
    p, c = lax.axis_index("pair"), lax.axis_index("ctx")
    own = p * ctxs + c
    slots = pairs * ctxs
    rows, later, size = q.shape[0], aq.shape[1], HEAD_SIZE
    cols = q.shape[1] // kv_heads
    group = cols // size
    scaling = size ** (-0.5)
    every = range(kv_heads)

    def peer(d):
        return lax.rem(c + d, ctxs)

    def partner(e):
        return lax.rem(p + e, pairs)

    loads = {}

    def load(h, index, src, dst):
        copy = pltpu.make_async_copy(src, dst, load_sem.at[h, index])
        copy.start()
        loads[h, index] = copy

    for h in every:
        narrow = pl.ds(h * size, size)
        load(h, 0, kp.at[:, narrow], gp.at[h, own, 0])
        load(h, 1, vp.at[:, narrow], gp.at[h, own, 1])
        load(h, 2, kr.at[0, :, narrow], gr.at[h, c, 0])
        load(h, 3, vr.at[0, :, narrow], gr.at[h, c, 1])
    for h in every:
        wide = pl.ds(h * cols, cols)
        load(h, 4, q.at[:, wide], q_v.at[h])
        load(h, 5, do.at[:, wide], do_v.at[h])
        load(h, 6, aq.at[0, :, wide], aq_v.at[h])
        load(h, 7, ado.at[0, :, wide], ado_v.at[h])
    greet(pairs, ctxs, p, c)

    across = {h: [] for h in every}
    replies = {h: [] for h in every}
    forwards = {h: [] for h in every}

    def send_keys(h):
        for i in range(4):
            loads[h, i].wait()
        own_slot, reply = gp.at[h, own], gr.at[h, c]
        for d in range(1, ctxs):
            across[h].append(
                remote(own_slot, own_slot, g_send.at[h, d - 1], g_recv.at[h, d - 1], {"ctx": peer(d)})
            )
        for e in range(1, pairs):
            forwards[h].append(
                remote(own_slot, own_slot, f_send.at[h, e - 1, 0], f_recv.at[h, e - 1, 0], {"pair": partner(e)})
            )
        for d in range(1, ctxs):
            replies[h].append(
                remote(reply, reply, r_send.at[h, d - 1], r_recv.at[h, d - 1], {"ctx": peer(d)})
            )

    def forward(h):
        for d in range(1, ctxs):
            across[h][d - 1].wait_recv()
            slot = gp.at[h, p * ctxs + lax.rem(c + ctxs - d, ctxs)]
            for e in range(1, pairs):
                forwards[h].append(
                    remote(slot, slot, f_send.at[h, e - 1, d], f_recv.at[h, e - 1, d], {"pair": partner(e)})
                )

    inner = {h: [] for h in every}
    outer = {h: [] for h in every}
    back = {h: [] for h in every}

    def send_terms(h):
        for d in list(range(1, ctxs)) + [0]:
            for e in range(1, pairs):
                inner[h].append((d, remote(
                    tp.at[h, partner(e) * ctxs + peer(d)], from_pair.at[h, e - 1, d],
                    x_send.at[h, e - 1, d], x_recv.at[h, e - 1, d], {"pair": partner(e)},
                )))

    def send_replies(h):
        tr[h, :, 0] = (kgrad_r[...] * scaling).astype(BF16).reshape(ctxs, later, size)
        tr[h, :, 1] = vgrad_r[...].astype(BF16).reshape(ctxs, later, size)
        for d in range(1, ctxs):
            back[h].append(remote(
                tr.at[h, peer(d)], from_reply.at[h, d - 1],
                z_send.at[h, d - 1], z_recv.at[h, d - 1], {"ctx": peer(d)},
            ))

    def pair_sum(h, d):
        total = tp[h, p * ctxs + peer(d)].astype(F32)
        for e in range(1, pairs):
            total = total + from_pair[h, e - 1, d].astype(F32)
        return total

    def pass_on(h):
        for d in range(1, ctxs):
            for at, copy in inner[h]:
                if at == d:
                    copy.wait_recv()
            summed[h, d - 1] = pair_sum(h, d).astype(BF16)
            outer[h].append(remote(
                summed.at[h, d - 1], from_ctx.at[h, d - 1],
                y_send.at[h, d - 1], y_recv.at[h, d - 1], {"ctx": peer(d)},
            ))

    stores = []

    def store(h, index, src, dst):
        copy = pltpu.make_async_copy(src, dst, store_sem.at[h, index])
        copy.start()
        stores.append(copy)

    def finish(h):
        narrow = slice(h * size, (h + 1) * size)
        for copy in back[h]:
            copy.wait_recv()
        total = tr[h, c].astype(F32)
        for d in range(1, ctxs):
            total = total + from_reply[h, d - 1].astype(F32)
        dkr[0, :, narrow] = total[0].astype(BF16)
        dvr[0, :, narrow] = total[1].astype(BF16)
        cut = pl.ds(h * size, size)
        store(h, 4, dkr.at[0, :, cut], dkr_h.at[0, :, cut])
        store(h, 5, dvr.at[0, :, cut], dvr_h.at[0, :, cut])
        for at, copy in inner[h]:
            if at == 0:
                copy.wait_recv()
        total = pair_sum(h, 0)
        for d in range(1, ctxs):
            outer[h][d - 1].wait_recv()
            total = total + from_ctx[h, d - 1].astype(F32)
        dkp[:, narrow] = total[0].astype(BF16)
        dvp[:, narrow] = total[1].astype(BF16)
        store(h, 6, dkp.at[:, cut], dkp_h.at[:, cut])
        store(h, 7, dvp.at[:, cut], dvp_h.at[:, cut])

    prompt_len = plen[0]
    answer_len = alen[p]
    prompt_first = own * rows
    answer_first = c * later

    def stacked(ref, h, heads):
        return jnp.concatenate([ref[h, :, i * size : (i + 1) * size] for i in heads], axis=0)

    send_keys(0)
    forward(0)
    for h in range(1, kv_heads):
        send_keys(h)
    for h in every:
        last = h + 1 == kv_heads
        for copy in forwards[h]:
            copy.wait_recv()
        keys = gp[h, :, 0].reshape(slots * rows, size)
        values = gp[h, :, 1].reshape(slots * rows, size)
        keys_t, values_t = keys.T, values.T
        for i in range(4, 8):
            loads[h, i].wait()
        fresh = True
        for answer in (True, False) if last else (False, True):
            if answer:
                for copy in replies[h]:
                    copy.wait_recv()
                keys_r = gr[h, :, 0].reshape(ctxs * later, size)
                values_r = gr[h, :, 1].reshape(ctxs * later, size)
                keys_rt, values_rt = keys_r.T, values_r.T
            count = later if answer else rows
            per_block = max(1, 256 // count)
            first = answer_first if answer else prompt_first
            live = answer_len if answer else prompt_len
            for start in range(0, group, per_block):
                heads = list(range(start, min(group, start + per_block)))
                lanes = len(heads) * count
                pos = row_positions(first, lanes, count)
                queries = stacked(aq_v if answer else q_v, h, heads)
                cotangent = stacked(ado_v if answer else do_v, h, heads)
                live_row = (
                    first
                    + lax.rem(lax.broadcasted_iota(jnp.int32, cotangent.shape, 0), jnp.int32(count))
                    < live
                )
                cotangent = jnp.where(live_row, cotangent.astype(F32), 0.0).astype(BF16)
                limit = jnp.minimum(pos, live - 1)
                if answer:
                    whole = jnp.full((1, lanes), prompt_len - 1, jnp.int32)
                    parts = [
                        (keys, values, keys_t, values_t, whole),
                        (keys_r, values_r, keys_rt, values_rt, limit),
                    ]
                    grads = [(kgrad, vgrad, fresh), (kgrad_r, vgrad_r, start == 0)]
                else:
                    parts = [(keys, values, keys_t, values_t, limit)]
                    grads = [(kgrad, vgrad, fresh)]
                o, g = attend_block(parts, queries, cotangent, pos < live, scaling, grads)
                o, g = o.T, g.T
                for i, k in enumerate(heads):
                    cut = slice(i * count, (i + 1) * count)
                    at = slice(h * cols + k * size, h * cols + (k + 1) * size)
                    if answer:
                        aout[0, :, at] = o[cut]
                        adq[0, :, at] = g[cut]
                    else:
                        out[:, at] = o[cut]
                        dq[:, at] = g[cut]
                if fresh:
                    if h > 0:
                        pass_on(h - 1)
                    if not last:
                        forward(h + 1)
                fresh = False
            if answer:
                send_replies(h)
        tp[h, :, 0] = (kgrad[...] * scaling).astype(BF16).reshape(slots, rows, size)
        tp[h, :, 1] = vgrad[...].astype(BF16).reshape(slots, rows, size)
        send_terms(h)
        wide = pl.ds(h * cols, cols)
        store(h, 0, out.at[:, wide], out_h.at[:, wide])
        store(h, 1, dq.at[:, wide], dq_h.at[:, wide])
        store(h, 2, aout.at[0, :, wide], aout_h.at[0, :, wide])
        store(h, 3, adq.at[0, :, wide], adq_h.at[0, :, wide])
        if h > 0:
            finish(h - 1)
    pass_on(kv_heads - 1)
    finish(kv_heads - 1)
    for h in every:
        for copy in across[h] + forwards[h] + replies[h] + outer[h] + back[h]:
            copy.wait_send()
        for _, copy in inner[h]:
            copy.wait_send()
    for copy in stores:
        copy.wait()


def fused(pairs, ctxs, q, kp, vp, aq, kr, vr, do, ado, plen, alen):
    size = HEAD_SIZE
    rows, width = kp.shape
    later = kr.shape[1]
    heads = width // size
    cols = q.shape[1] // heads
    slots = pairs * ctxs
    smem = pl.BlockSpec(memory_space=pltpu.SMEM)
    hbm = pl.BlockSpec(memory_space=pltpu.HBM)
    dma = pltpu.SemaphoreType.DMA
    like = lambda x: jax.ShapeDtypeStruct(x.shape, BF16)
    wide = pltpu.VMEM((heads, rows, cols), BF16)
    wide_r = pltpu.VMEM((heads, later, cols), BF16)
    terms = pltpu.VMEM((heads, slots, 2, rows, size), BF16)
    terms_r = pltpu.VMEM((heads, ctxs, 2, later, size), BF16)
    return pl.pallas_call(
        functools.partial(fused_kernel, pairs, ctxs, heads),
        out_shape=tuple(map(like, (q, aq, q, kp, vp, aq, kr, vr))),
        in_specs=[smem] * 2 + [hbm] * 8,
        out_specs=(hbm,) * 8,
        scratch_shapes=[
            terms, terms_r, wide, wide_r, wide, wide_r,
            *[pltpu.VMEM(x.shape, BF16) for x in (q, aq, q, kp, vp, aq, kr, vr)],
            pltpu.VMEM((slots * rows, size), F32),
            pltpu.VMEM((slots * rows, size), F32),
            pltpu.VMEM((ctxs * later, size), F32),
            pltpu.VMEM((ctxs * later, size), F32),
            terms, terms_r,
            pltpu.VMEM((heads, pairs - 1, ctxs, 2, rows, size), BF16),
            pltpu.VMEM((heads, ctxs - 1, 2, rows, size), BF16),
            pltpu.VMEM((heads, ctxs - 1, 2, later, size), BF16),
            pltpu.VMEM((heads, ctxs - 1, 2, rows, size), BF16),
            dma((heads, 8)), dma((heads, 8)),
            dma((heads, ctxs - 1)), dma((heads, ctxs - 1)),
            dma((heads, ctxs - 1)), dma((heads, ctxs - 1)),
            dma((heads, pairs - 1, ctxs)), dma((heads, pairs - 1, ctxs)),
            dma((heads, pairs - 1, ctxs)), dma((heads, pairs - 1, ctxs)),
            dma((heads, ctxs - 1)), dma((heads, ctxs - 1)),
            dma((heads, ctxs - 1)), dma((heads, ctxs - 1)),
        ],
        compiler_params=pltpu.CompilerParams(
            collective_id=0, has_side_effects=True, vmem_limit_bytes=56 * 2**20
        ),
    )(plen, alen, q, kp, vp, aq, kr, vr, do, ado)


def hand_on_kernel(count, *refs):
    sources, targets, held = refs[:count], refs[count : 2 * count], refs[2 * count : 3 * count]
    sems = refs[-1]
    ins = [pltpu.make_async_copy(sources[i], held[i], sems.at[0, i]) for i in range(count)]
    outs = [pltpu.make_async_copy(held[i], targets[i], sems.at[1, i]) for i in range(count)]
    for copy in ins:
        copy.start()
    for i in range(count):
        ins[i].wait()
        outs[i].start()
    for copy in outs:
        copy.wait()


def hand_on(arrays):
    hbm = pl.BlockSpec(memory_space=pltpu.HBM)
    count = len(arrays)
    return pl.pallas_call(
        functools.partial(hand_on_kernel, count),
        out_shape=tuple(jax.ShapeDtypeStruct(x.shape, x.dtype) for x in arrays),
        in_specs=[hbm] * count,
        out_specs=(hbm,) * count,
        scratch_shapes=[pltpu.VMEM(x.shape, x.dtype) for x in arrays]
        + [pltpu.SemaphoreType.DMA((2, count))],
        compiler_params=pltpu.CompilerParams(vmem_limit_bytes=56 * 2**20),
    )(*arrays)


def body(pairs, ctxs, *operands):
    return hand_on(fused(pairs, ctxs, *operands))


def solution(mesh):
    flat = P(("pair", "ctx"), "head")
    deep = P("pair", "ctx", "head")
    return jax.shard_map(
        functools.partial(body, mesh.shape["pair"], mesh.shape["ctx"]),
        mesh=mesh,
        in_specs=(flat, flat, flat, deep, deep, deep, flat, deep, P(), P()),
        out_specs=(flat, deep, flat, flat, flat, deep, deep, deep),
        check_vma=False,
    )
```

```python
import functools
import math

import jax
import jax.numpy as jnp
from jax import lax
from jax.experimental import pallas as pl
from jax.experimental.pallas import tpu as pltpu
from jax.sharding import PartitionSpec as P

KEY_VALUE_HEADS = 8
HEAD_SIZE = 128
NEGATIVE = -1e30
MESH = pl.DeviceIdType.MESH
F32 = jnp.float32
BF16 = jnp.bfloat16


def greet(pairs, ctxs, p, c):
    barrier = pltpu.get_barrier_semaphore()
    for e in range(1, pairs):
        pl.semaphore_signal(
            barrier, inc=1, device_id={"pair": lax.rem(p + e, pairs)}, device_id_type=MESH
        )
    for d in range(1, ctxs):
        pl.semaphore_signal(
            barrier, inc=1, device_id={"ctx": lax.rem(c + d, ctxs)}, device_id_type=MESH
        )
    pl.semaphore_wait(barrier, pairs + ctxs - 2)


def dot(a, b):
    return lax.dot_general(a, b, (((1,), (0,)), ((), ())), preferred_element_type=F32)


def dot_nt(a, b):
    return lax.dot_general(a, b, (((1,), (1,)), ((), ())), preferred_element_type=F32)


def row_positions(first, count, rows):
    lane = lax.broadcasted_iota(jnp.int32, (1, count), 1)
    return first + lax.rem(lane, jnp.int32(rows))


def first_products(parts, queries, cotangent):
    scores = []
    top = None
    for keys, _, _, _, limit in parts:
        s = dot_nt(keys, queries)
        at = lax.broadcasted_iota(jnp.int32, s.shape, 0)
        s = jnp.where(at <= limit, s, NEGATIVE)
        m = jnp.max(s, axis=0, keepdims=True)
        top = m if top is None else jnp.maximum(top, m)
        scores.append(s)
    return scores, top, [dot_nt(part[1], cotangent) for part in parts]


def attend_block(parts, queries, cotangent, valid, scaling, grads, products):
    factor = scaling * math.log2(math.e)
    scores, top, prob_grads = products
    terms = [jnp.exp2((s - top) * factor) for s in scores]
    total = sum(jnp.sum(t, axis=0, keepdims=True) for t in terms)
    inverse = 1.0 / total
    output = sum(dot(part[3], t.astype(BF16)) for part, t in zip(parts, terms))
    output = jnp.where(valid, output * inverse, 0.0).astype(BF16)
    shares = [t * inverse for t in terms]
    delta = sum(jnp.sum(w * g, axis=0, keepdims=True) for w, g in zip(shares, prob_grads))
    query_grad = None
    for part, w, g, (key_grad, value_grad, fresh) in zip(parts, shares, prob_grads, grads):
        value_add = dot(w.astype(BF16), cotangent)
        score_grad = (w * (g - delta)).astype(BF16)
        key_add = dot(score_grad, queries)
        if fresh:
            value_grad[...] = value_add
            key_grad[...] = key_add
        else:
            value_grad[...] += value_add
            key_grad[...] += key_add
        add = dot(part[2], score_grad)
        query_grad = add if query_grad is None else query_grad + add
    return output, (query_grad * scaling).astype(BF16)


def remote(src, dst, send, recv, device):
    copy = pltpu.make_async_remote_copy(
        src_ref=src, dst_ref=dst, send_sem=send, recv_sem=recv, device_id=device, device_id_type=MESH
    )
    copy.start()
    return copy


def fused_kernel(
    pairs, ctxs, kv_heads,
    plen, alen, q, kp, vp, aq, kr, vr, do, ado,
    out_h, aout_h, dq_h, dkp_h, dvp_h, adq_h, dkr_h, dvr_h,
    gp, gr, q_v, aq_v, do_v, ado_v,
    out, aout, dq, dkp, dvp, adq, dkr, dvr,
    kgrad, vgrad, kgrad_r, vgrad_r, tp, tr, from_pair, from_ctx, from_reply, summed,
    load_sem, store_sem,
    g_send, g_recv, r_send, r_recv, f_send, f_recv,
    x_send, x_recv, y_send, y_recv, z_send, z_recv,
):
    p, c = lax.axis_index("pair"), lax.axis_index("ctx")
    own = p * ctxs + c
    slots = pairs * ctxs
    rows, later, size = q.shape[0], aq.shape[1], HEAD_SIZE
    cols = q.shape[1] // kv_heads
    group = cols // size
    scaling = size ** (-0.5)
    every = range(kv_heads)

    def peer(d):
        return lax.rem(c + d, ctxs)

    def partner(e):
        return lax.rem(p + e, pairs)

    loads = {}

    def load(h, index, src, dst):
        copy = pltpu.make_async_copy(src, dst, load_sem.at[h, index])
        copy.start()
        loads[h, index] = copy

    for h in every:
        narrow = pl.ds(h * size, size)
        load(h, 0, kp.at[:, narrow], gp.at[h, own, 0])
        load(h, 1, vp.at[:, narrow], gp.at[h, own, 1])
        load(h, 2, kr.at[0, :, narrow], gr.at[h, c, 0])
        load(h, 3, vr.at[0, :, narrow], gr.at[h, c, 1])
    for h in every:
        wide = pl.ds(h * cols, cols)
        load(h, 4, q.at[:, wide], q_v.at[h])
        load(h, 5, do.at[:, wide], do_v.at[h])
        load(h, 6, aq.at[0, :, wide], aq_v.at[h])
        load(h, 7, ado.at[0, :, wide], ado_v.at[h])
    greet(pairs, ctxs, p, c)

    across = {h: [] for h in every}
    replies = {h: [] for h in every}
    forwards = {h: [] for h in every}

    def send_keys(h):
        for i in range(4):
            loads[h, i].wait()
        own_slot, reply = gp.at[h, own], gr.at[h, c]
        for d in range(1, ctxs):
            across[h].append(
                remote(own_slot, own_slot, g_send.at[h, d - 1], g_recv.at[h, d - 1], {"ctx": peer(d)})
            )
        for e in range(1, pairs):
            forwards[h].append(
                remote(own_slot, own_slot, f_send.at[h, e - 1, 0], f_recv.at[h, e - 1, 0], {"pair": partner(e)})
            )
        for d in range(1, ctxs):
            replies[h].append(
                remote(reply, reply, r_send.at[h, d - 1], r_recv.at[h, d - 1], {"ctx": peer(d)})
            )

    def forward(h):
        for d in range(1, ctxs):
            across[h][d - 1].wait_recv()
            slot = gp.at[h, p * ctxs + lax.rem(c + ctxs - d, ctxs)]
            for e in range(1, pairs):
                forwards[h].append(
                    remote(slot, slot, f_send.at[h, e - 1, d], f_recv.at[h, e - 1, d], {"pair": partner(e)})
                )

    inner = {h: [] for h in every}
    outer = {h: [] for h in every}
    back = {h: [] for h in every}

    def send_terms(h):
        for d in list(range(1, ctxs)) + [0]:
            for e in range(1, pairs):
                inner[h].append((d, remote(
                    tp.at[h, partner(e) * ctxs + peer(d)], from_pair.at[h, e - 1, d],
                    x_send.at[h, e - 1, d], x_recv.at[h, e - 1, d], {"pair": partner(e)},
                )))

    def send_replies(h):
        tr[h, :, 0] = (kgrad_r[...] * scaling).astype(BF16).reshape(ctxs, later, size)
        tr[h, :, 1] = vgrad_r[...].astype(BF16).reshape(ctxs, later, size)
        for d in range(1, ctxs):
            back[h].append(remote(
                tr.at[h, peer(d)], from_reply.at[h, d - 1],
                z_send.at[h, d - 1], z_recv.at[h, d - 1], {"ctx": peer(d)},
            ))

    def pair_sum(h, d):
        total = tp[h, p * ctxs + peer(d)].astype(F32)
        for e in range(1, pairs):
            total = total + from_pair[h, e - 1, d].astype(F32)
        return total

    def pass_on(h):
        for d in range(1, ctxs):
            for at, copy in inner[h]:
                if at == d:
                    copy.wait_recv()
            summed[h, d - 1] = pair_sum(h, d).astype(BF16)
            outer[h].append(remote(
                summed.at[h, d - 1], from_ctx.at[h, d - 1],
                y_send.at[h, d - 1], y_recv.at[h, d - 1], {"ctx": peer(d)},
            ))

    stores = []

    def store(h, index, src, dst):
        copy = pltpu.make_async_copy(src, dst, store_sem.at[h, index])
        copy.start()
        stores.append(copy)

    def finish(h):
        narrow = slice(h * size, (h + 1) * size)
        for copy in back[h]:
            copy.wait_recv()
        total = tr[h, c].astype(F32)
        for d in range(1, ctxs):
            total = total + from_reply[h, d - 1].astype(F32)
        dkr[0, :, narrow] = total[0].astype(BF16)
        dvr[0, :, narrow] = total[1].astype(BF16)
        cut = pl.ds(h * size, size)
        store(h, 4, dkr.at[0, :, cut], dkr_h.at[0, :, cut])
        store(h, 5, dvr.at[0, :, cut], dvr_h.at[0, :, cut])
        for at, copy in inner[h]:
            if at == 0:
                copy.wait_recv()
        total = pair_sum(h, 0)
        for d in range(1, ctxs):
            outer[h][d - 1].wait_recv()
            total = total + from_ctx[h, d - 1].astype(F32)
        dkp[:, narrow] = total[0].astype(BF16)
        dvp[:, narrow] = total[1].astype(BF16)
        store(h, 6, dkp.at[:, cut], dkp_h.at[:, cut])
        store(h, 7, dvp.at[:, cut], dvp_h.at[:, cut])

    prompt_len = plen[0]
    answer_len = alen[p]
    prompt_first = own * rows
    answer_first = c * later

    def stacked(ref, h, heads):
        return jnp.concatenate([ref[h, :, i * size : (i + 1) * size] for i in heads], axis=0)

    send_keys(0)
    forward(0)
    for h in range(1, kv_heads):
        send_keys(h)
    for h in every:
        last = h + 1 == kv_heads
        for copy in forwards[h]:
            copy.wait_recv()
        keys = gp[h, :, 0].reshape(slots * rows, size)
        values = gp[h, :, 1].reshape(slots * rows, size)
        keys_t, values_t = keys.T, values.T
        for i in range(4, 8):
            loads[h, i].wait()
        fresh = True
        for answer in (True, False) if last else (False, True):
            blocks = []
            if answer:
                for copy in replies[h]:
                    copy.wait_recv()
                keys_r = gr[h, :, 0].reshape(ctxs * later, size)
                values_r = gr[h, :, 1].reshape(ctxs * later, size)
                keys_rt, values_rt = keys_r.T, values_r.T
            count = later if answer else rows
            per_block = max(1, 256 // count)
            first = answer_first if answer else prompt_first
            live = answer_len if answer else prompt_len
            live_row = first + lax.broadcasted_iota(jnp.int32, (count, size), 0) < live
            q_ref, do_ref = (aq_v, ado_v) if answer else (q_v, do_v)
            for start in range(0, group, per_block):
                heads = list(range(start, min(group, start + per_block)))
                lanes = len(heads) * count
                pos = row_positions(first, lanes, count)
                limit = jnp.minimum(pos, live - 1)
                if answer:
                    whole = jnp.full((1, lanes), prompt_len - 1, jnp.int32)
                    parts = [
                        (keys, values, keys_t, values_t, whole),
                        (keys_r, values_r, keys_rt, values_rt, limit),
                    ]
                else:
                    parts = [(keys, values, keys_t, values_t, limit)]
                blocks.append((start, heads, pos, parts))

            def begin(index):
                _, heads, _, parts = blocks[index]
                queries = stacked(q_ref, h, heads)
                cotangent = jnp.concatenate(
                    [
                        jnp.where(live_row, do_ref[h, :, i * size : (i + 1) * size].astype(F32), 0.0)
                        for i in heads
                    ],
                    axis=0,
                ).astype(BF16)
                return queries, cotangent, first_products(parts, queries, cotangent)

            ahead = begin(0)
            for index, (start, heads, pos, parts) in enumerate(blocks):
                queries, cotangent, products = ahead
                if index + 1 < len(blocks):
                    ahead = begin(index + 1)
                grads = [(kgrad, vgrad, fresh)]
                if answer:
                    grads.append((kgrad_r, vgrad_r, start == 0))
                o, g = attend_block(
                    parts, queries, cotangent, pos < live, scaling, grads, products
                )
                o, g = o.T, g.T
                for i, k in enumerate(heads):
                    cut = slice(i * count, (i + 1) * count)
                    at = slice(h * cols + k * size, h * cols + (k + 1) * size)
                    if answer:
                        aout[0, :, at] = o[cut]
                        adq[0, :, at] = g[cut]
                    else:
                        out[:, at] = o[cut]
                        dq[:, at] = g[cut]
                if fresh:
                    if h > 0:
                        pass_on(h - 1)
                    if not last:
                        forward(h + 1)
                fresh = False
            if answer:
                send_replies(h)
        tp[h, :, 0] = (kgrad[...] * scaling).astype(BF16).reshape(slots, rows, size)
        tp[h, :, 1] = vgrad[...].astype(BF16).reshape(slots, rows, size)
        send_terms(h)
        wide = pl.ds(h * cols, cols)
        store(h, 0, out.at[:, wide], out_h.at[:, wide])
        store(h, 1, dq.at[:, wide], dq_h.at[:, wide])
        store(h, 2, aout.at[0, :, wide], aout_h.at[0, :, wide])
        store(h, 3, adq.at[0, :, wide], adq_h.at[0, :, wide])
        if h > 0:
            finish(h - 1)
    pass_on(kv_heads - 1)
    finish(kv_heads - 1)
    for h in every:
        for copy in across[h] + forwards[h] + replies[h] + outer[h] + back[h]:
            copy.wait_send()
        for _, copy in inner[h]:
            copy.wait_send()
    for copy in stores:
        copy.wait()


def fused(pairs, ctxs, q, kp, vp, aq, kr, vr, do, ado, plen, alen):
    size = HEAD_SIZE
    rows, width = kp.shape
    later = kr.shape[1]
    heads = width // size
    cols = q.shape[1] // heads
    slots = pairs * ctxs
    smem = pl.BlockSpec(memory_space=pltpu.SMEM)
    hbm = pl.BlockSpec(memory_space=pltpu.HBM)
    dma = pltpu.SemaphoreType.DMA
    like = lambda x: jax.ShapeDtypeStruct(x.shape, BF16)
    wide = pltpu.VMEM((heads, rows, cols), BF16)
    wide_r = pltpu.VMEM((heads, later, cols), BF16)
    terms = pltpu.VMEM((heads, slots, 2, rows, size), BF16)
    terms_r = pltpu.VMEM((heads, ctxs, 2, later, size), BF16)
    return pl.pallas_call(
        functools.partial(fused_kernel, pairs, ctxs, heads),
        out_shape=tuple(map(like, (q, aq, q, kp, vp, aq, kr, vr))),
        in_specs=[smem] * 2 + [hbm] * 8,
        out_specs=(hbm,) * 8,
        scratch_shapes=[
            terms, terms_r, wide, wide_r, wide, wide_r,
            *[pltpu.VMEM(x.shape, BF16) for x in (q, aq, q, kp, vp, aq, kr, vr)],
            pltpu.VMEM((slots * rows, size), F32),
            pltpu.VMEM((slots * rows, size), F32),
            pltpu.VMEM((ctxs * later, size), F32),
            pltpu.VMEM((ctxs * later, size), F32),
            terms, terms_r,
            pltpu.VMEM((heads, pairs - 1, ctxs, 2, rows, size), BF16),
            pltpu.VMEM((heads, ctxs - 1, 2, rows, size), BF16),
            pltpu.VMEM((heads, ctxs - 1, 2, later, size), BF16),
            pltpu.VMEM((heads, ctxs - 1, 2, rows, size), BF16),
            dma((heads, 8)), dma((heads, 8)),
            dma((heads, ctxs - 1)), dma((heads, ctxs - 1)),
            dma((heads, ctxs - 1)), dma((heads, ctxs - 1)),
            dma((heads, pairs - 1, ctxs)), dma((heads, pairs - 1, ctxs)),
            dma((heads, pairs - 1, ctxs)), dma((heads, pairs - 1, ctxs)),
            dma((heads, ctxs - 1)), dma((heads, ctxs - 1)),
            dma((heads, ctxs - 1)), dma((heads, ctxs - 1)),
        ],
        compiler_params=pltpu.CompilerParams(
            collective_id=0, has_side_effects=True, vmem_limit_bytes=56 * 2**20
        ),
    )(plen, alen, q, kp, vp, aq, kr, vr, do, ado)


def hand_on_kernel(count, *refs):
    sources, targets, held = refs[:count], refs[count : 2 * count], refs[2 * count : 3 * count]
    sems = refs[-1]
    ins = [pltpu.make_async_copy(sources[i], held[i], sems.at[0, i]) for i in range(count)]
    outs = [pltpu.make_async_copy(held[i], targets[i], sems.at[1, i]) for i in range(count)]
    for copy in ins:
        copy.start()
    for i in range(count):
        ins[i].wait()
        outs[i].start()
    for copy in outs:
        copy.wait()


def hand_on(arrays):
    hbm = pl.BlockSpec(memory_space=pltpu.HBM)
    count = len(arrays)
    return pl.pallas_call(
        functools.partial(hand_on_kernel, count),
        out_shape=tuple(jax.ShapeDtypeStruct(x.shape, x.dtype) for x in arrays),
        in_specs=[hbm] * count,
        out_specs=(hbm,) * count,
        scratch_shapes=[pltpu.VMEM(x.shape, x.dtype) for x in arrays]
        + [pltpu.SemaphoreType.DMA((2, count))],
        compiler_params=pltpu.CompilerParams(vmem_limit_bytes=56 * 2**20),
    )(*arrays)


def body(pairs, ctxs, *operands):
    return hand_on(fused(pairs, ctxs, *operands))


def solution(mesh):
    flat = P(("pair", "ctx"), "head")
    deep = P("pair", "ctx", "head")
    return jax.shard_map(
        functools.partial(body, mesh.shape["pair"], mesh.shape["ctx"]),
        mesh=mesh,
        in_specs=(flat, flat, flat, deep, deep, deep, flat, deep, P(), P()),
        out_specs=(flat, deep, flat, flat, flat, deep, deep, deep),
        check_vma=False,
    )
```
